512 devices in a mesh: group: 8 (over x, z_lo), space: 64 (over y, z_hi, core).
Axes of the slice: x: 4, y: 8, z: 8 (z_hi: 4, z_lo: 2; z = z_hi * 2 + z_lo), core: 2. Of those that a mesh axis runs over, the one named last changes fastest.
Arguments:
- pressure_prev: float32 [8, 512, 128, 256], P('group', 'space'), may hold values from -6 to 6
- pressure_now: float32 [8, 512, 128, 256], P('group', 'space'), may hold values from -6 to 6
- regions: int32 [512, 128, 256], P('space'), may hold values from 0 to 15
- speed_table: float32 [16], replicated, may hold values from 0.02 to 0.18
- image: float32 [512, 64, 128], P('space', 'group'), may hold values from -6 to 6
- box: int32 [2], replicated, may hold values from 0 to 64, as said below
Outputs:
- out_prev: float32 [8, 512, 128, 256], P('group', 'space')
- out_now: float32 [8, 512, 128, 256], P('group', 'space')
- out_image: float32 [512, 64, 128], P('space', 'group')
The draws below stay inside these ranges and needn't reach their ends.
Inputs may be any that keep to these rules, and one draw needn't show every extreme that they name: box[0] + 64 <= 128 and box[1] + 128 <= 256; the two entries differ, and one of them equals min(64, 128).
All inputs are finite; a program needn't handle non-finite values.
Results may differ from the reference program's by a relative error of at most 0.00002.
Values sent between devices are 32-bit elements; how exact they have to be, the bound alone decides.
No kernel may reach another device: no remote copies, remote signals or barrier semaphores. Data moves between devices by JAX's collectives and lax.ppermute only.
A program may use at most 64 MiB of HBM per device.

```python
import math
import jax
import jax.numpy as jnp
from jax import lax

NY = 128
NZ = 256
ZY = 64
ZZ = 128
REGIONS = 16
STEPS = 4
GROUPS = 8
NX = 512


def draw_box(key, part):
    key = jax.random.fold_in(key, 11)
    other_key, side_key = jax.random.split(key)
    top = min(NY - ZY, NZ - ZZ)
    other = jax.random.randint(other_key, (), 0, top, dtype=jnp.int32)
    side = jax.random.randint(side_key, (), 0, 2, dtype=jnp.int32)
    upper = jnp.int32(top)
    first = jnp.where(side == 0, upper, other)
    second = jnp.where(side == 0, other, upper)
    return jnp.stack([first, second]).astype(jnp.int32)


def touch_ends(drawn, rng, least, top_value):
    longest = drawn.shape.index(max(drawn.shape))
    spots = []
    for shift in (0, 1):
        where = [jax.random.randint(jax.random.fold_in(rng, axis), (), 0, length) for axis, length in enumerate(drawn.shape)]
        where[longest] = (where[longest] + shift) % drawn.shape[longest]
        spots.append(tuple(where))
    return drawn.at[spots[0]].set(least).at[spots[1]].set(top_value)


def level_of(own_key, shape, shards, least, high):
    def one(axis_at, shards_of):
        draws = jax.random.uniform(jax.random.fold_in(jax.random.fold_in(own_key, 6), axis_at), (shards_of,), jnp.float32, least / len(shards), high / len(shards))
        return jnp.repeat(jnp.exp(draws), shape[axis_at] // shards_of).reshape((-1,) + (1,) * (len(shape) - axis_at - 1))

    level = one(*shards[0])
    for cut in shards[1:]:
        level = level * one(*cut)
    return level


def normal_values(own_key, extent, spread, bound, cuts=(), kind=jnp.bfloat16):
    drawn = jax.random.normal(own_key, extent, jnp.float32) * spread
    if len(cuts) > 0:
        drawn = level_of(own_key, extent, cuts, -0.22, 0.18) * drawn
    return jnp.clip(drawn, min=-bound, max=bound).astype(kind)


def setup_inputs(seed: int = 0) -> dict:
    key_of = jax.random.split(jax.random.key(seed), 7)
    return {
        "pressure_prev": normal_values(key_of[0], (GROUPS, NX, NY, NZ), 1.0, 6.0, ((0, 8), (1, 64)), jnp.float32),
        "pressure_now": normal_values(key_of[1], (GROUPS, NX, NY, NZ), 1.0, 6.0, ((0, 8), (1, 64)), jnp.float32),
        "regions": touch_ends(jax.random.randint(key_of[2], (NX, NY, NZ), 0, REGIONS), jax.random.fold_in(key_of[2], 1), 0, REGIONS - 1).astype(jnp.int32),
        "speed_table": jnp.clip(jnp.exp(jax.random.uniform(key_of[3], (REGIONS,), jnp.float32, math.log(0.02), math.log(0.18))), 0.02, 0.18),
        "image": normal_values(key_of[4], (NX, ZY, ZZ), 1.0, 6.0, ((0, 64), (1, 8)), jnp.float32),
        "box": draw_box(jax.random.fold_in(key_of[6], 71), 0),
    }


coeffs = (-205.0 / 72.0, 8.0 / 5.0, -1.0 / 5.0, 8.0 / 315.0, -1.0 / 560.0)


def laplace(extended):
    rows = extended.shape[0] - 8
    centre = extended[4:4 + rows]
    total = 3.0 * coeffs[0] * centre
    for k in range(1, 5):
        total = total + coeffs[k] * (extended[4 + k:4 + k + rows] + extended[4 - k:4 - k + rows])
    padded = jnp.pad(centre, ((0, 0), (4, 4), (4, 4)))
    ny = centre.shape[1]
    nz = centre.shape[2]
    for k in range(1, 5):
        total = total + coeffs[k] * (padded[:, 4 + k:4 + k + ny, 4:4 + nz] + padded[:, 4 - k:4 - k + ny, 4:4 + nz])
        total = total + coeffs[k] * (padded[:, 4:4 + ny, 4 + k:4 + k + nz] + padded[:, 4:4 + ny, 4 - k:4 - k + nz])
    return total


def reference(pressure_prev, pressure_now, regions, speed_table, image, box):
    coef = speed_table[regions]
    prev, now = pressure_prev, pressure_now

    def advance(pair):
        older, field = pair
        extended = jnp.pad(field, ((4, 4), (0, 0), (0, 0)))
        return 2.0 * field - older + coef * laplace(extended)

    total = image
    for step in range(STEPS):
        nxt = lax.map(advance, (prev, now))
        prev, now = now, nxt
        zone = lax.dynamic_slice(now, (jnp.int32(0), jnp.int32(0), box[0].astype(jnp.int32), box[1].astype(jnp.int32)), (GROUPS, NX, ZY, ZZ))
        total = total + jnp.prod(zone, axis=0)
    return prev, now, total
```

```python
import functools

import jax
import jax.numpy as jnp
from jax import lax
from jax.experimental import pallas as pl
from jax.experimental.pallas import tpu as pltpu
from jax.sharding import PartitionSpec as P

STEPS = 4
SCALE = 5040.0
CENTRE = -3.0 * 14350.0
TAPS = (8064.0, -1008.0, 128.0, -9.0)
PLANES, NY, NZ = 8, 128, 256
FACE = 4
HALVES = 2
ROWS = NY // HALVES
ZY, ZZ = 64, 128
GROUPS = 8
VMEM_LIMIT = 16 * 1024 * 1024
COST = (1, 10**10, 1, 10**10)
F32 = jnp.float32
BF16 = jnp.bfloat16

VM = pl.BlockSpec(memory_space=pltpu.VMEM)
SM = pl.BlockSpec(memory_space=pltpu.SMEM)
ANY = pl.BlockSpec(memory_space=pl.ANY)


def band(size):
    apart = jnp.abs(
        lax.broadcasted_iota(jnp.int32, (size, size), 0)
        - lax.broadcasted_iota(jnp.int32, (size, size), 1)
    )
    matrix = jnp.zeros((size, size), F32)
    for k, tap in enumerate(TAPS, 1):
        matrix = jnp.where(apart == k, tap, matrix)
    return matrix.astype(BF16)


def store_bands(across_y, across_z):
    along_y, along_z = band(NY), band(NZ)
    for i in range(3):
        across_y[:, i * NY : (i + 1) * NY] = along_y
        across_z[i * NZ : (i + 1) * NZ, :] = along_z


def call(kernel, outs, in_specs, out_specs, args, cost=1, scratch=(), aliases=None):
    return pl.pallas_call(
        kernel,
        out_shape=[jax.ShapeDtypeStruct(shape, F32) for shape in outs],
        in_specs=in_specs,
        out_specs=out_specs,
        scratch_shapes=list(scratch),
        input_output_aliases=aliases or {},
        compiler_params=pltpu.CompilerParams(vmem_limit_bytes=VMEM_LIMIT),
        cost_estimate=pl.CostEstimate(flops=cost, bytes_accessed=cost, transcendentals=0),
    )(*args)


def thirds(x):
    high = x.astype(BF16)
    left = x - high.astype(F32)
    middle = left.astype(BF16)
    low = (left - middle.astype(F32)).astype(BF16)
    return high, middle, low


def cross_terms(plane, across_y, across_z):
    pieces = thirds(plane)
    along_z = jnp.dot(
        jnp.concatenate(pieces, axis=1), across_z, preferred_element_type=F32
    )
    along_y = jnp.dot(
        across_y, jnp.concatenate(pieces, axis=0), preferred_element_type=F32
    )
    return along_z + along_y


def advance(now, older, coef_of, cross, store_base, store_next):
    for half in range(HALVES):

        @pl.loop(0, ROWS // 8)
        def _(block):
            inner = pl.ds(pl.multiple_of(block * 8, 8), 8)
            outer = pl.ds(pl.multiple_of(half * ROWS + block * 8, 8), 8)
            at = (inner, outer, half)
            values = [now(j, at) for j in range(PLANES)]
            for j in range(PLANES):
                total = cross[j, outer, :] + CENTRE * values[j]
                for k, tap in enumerate(TAPS, 1):
                    pair = [values[i] for i in (j + k, j - k) if 0 <= i < len(values)]
                    if pair:
                        total = total + tap * sum(pair[1:], pair[0])
                value = 2.0 * values[j] - older(j, at) + coef_of(j, at) * total
                if j < FACE:
                    store_base(j, at, value)
                else:
                    store_next(j - FACE, at, value)


def from_natural(ref, flip):
    return lambda j, at: ref[j ^ flip, at[1], :]


def from_parts(first, second, rest):
    def rows(j, at):
        if j >= FACE:
            return rest[j - FACE, at[1], :]
        return (first, second)[at[2]][j, at[0], :]

    return rows


def whole_plane(first, second, rest, j):
    if j >= FACE:
        return rest[j - FACE]
    return jnp.concatenate([first[j], second[j]], axis=0)


def cut_zone(plane, box):
    moved = pltpu.roll(plane, (NY - box[0]) % NY, 0)[:ZY]
    return pltpu.roll(moved, (NZ - box[1]) % NZ, 1)[:, :ZZ]


def split_zone(plane, box):
    return cut_zone(plane, box).reshape(GROUPS, ZY // GROUPS, ZZ)


def put_rows(ref):
    def put(j, at, value):
        ref[j, at[1], :] = value

    return put


def first_kernel(place, table, now, prev, regions, coef, base, rest, cross, across_y, across_z):
    flip = place[0]
    store_bands(across_y, across_z)
    scaled = [table[i] * (1.0 / SCALE) for i in range(16)]
    for j in range(PLANES):
        cross[j] = cross_terms(now[j ^ flip], across_y[...], across_z[...])

    def coef_of(j, at):
        code = regions[j ^ flip, at[1], :]
        level = scaled
        for bit in range(4):
            odd = (code & (1 << bit)) != 0
            level = [
                jnp.where(odd, level[2 * i + 1], level[2 * i]) for i in range(len(level) // 2)
            ]
        coef[j, at[1], :] = level[0]
        return level[0]

    advance(
        from_natural(now, flip),
        from_natural(prev, flip),
        coef_of,
        cross,
        put_rows(base),
        put_rows(rest),
    )


def middle_kernel(first, place, box, n1, n2, partial, halo, *refs):
    *refs, now, base, nxt, zones, cross, across_y, across_z = refs
    if first:
        prev, coef = refs
        older = from_natural(prev, place[0])
        earlier = ()
    else:
        p1, p2, pa, coef, *earlier = refs
        older = from_parts(p1, p2, pa)
    for zone in earlier:
        zones[:, : zone.shape[1]] = zone[...]
    far_terms(coef, partial, halo, 3 - place[1] if first else 0, now)
    store_bands(across_y, across_z)
    for j in range(PLANES):
        plane = whole_plane(n1, n2, now, j)
        cross[j] = cross_terms(plane, across_y[...], across_z[...])
        zones[:, zones.shape[1] - 1, j] = split_zone(plane, box)
    advance(
        from_parts(n1, n2, now),
        older,
        lambda j, at: coef[j, at[1], :],
        cross,
        put_rows(base),
        put_rows(nxt),
    )


def face_terms(base, coef, halo, turn, half, put):
    @pl.loop(0, ROWS // 8)
    def _(block):
        inner = pl.ds(pl.multiple_of(block * 8, 8), 8)
        outer = pl.ds(pl.multiple_of(half * ROWS + block * 8, 8), 8)
        beyond = [halo[k ^ turn, inner, :] for k in range(FACE)]
        for j in range(FACE):
            total = TAPS[j] * beyond[0]
            for k in range(1, FACE - j):
                total = total + TAPS[j + k] * beyond[k]
            put(j, inner, base[j, outer, :] + coef[j, outer, :] * total)


def face_kernel(half, first, place, base, coef, halo, *refs):
    out = refs[2 if half else 0]
    turn = 3 - place[1] if first else 0

    def put(j, inner, value):
        out[j, inner, :] = value

    face_terms(base, coef, halo, turn, half, put)


def far_terms(coef, partial, halo, turn, out):
    @pl.loop(0, NY // 8)
    def _(block):
        rows = pl.ds(pl.multiple_of(block * 8, 8), 8)
        beyond = [halo[(FACE - 1 - k) ^ turn, rows, :] for k in range(FACE)]
        for j in range(FACE):
            total = TAPS[j] * beyond[0]
            for k in range(1, FACE - j):
                total = total + TAPS[j + k] * beyond[k]
            mine = FACE - 1 - j
            out[mine, rows, :] = partial[mine, rows, :] + coef[FACE + mine, rows, :] * total


def last_kernel(box, base, coef, halo, n1, partial, far_halo, earlier, n2, now, zones):
    def put(j, inner, value):
        n2[j, inner, :] = value

    face_terms(base, coef, halo, 0, 1, put)
    far_terms(coef, partial, far_halo, 0, now)
    zones[:, : STEPS - 1] = earlier[...]
    for j in range(PLANES):
        zones[:, STEPS - 1, j] = split_zone(whole_plane(n1, n2, now, j), box)


def gather_kernel(place, n1, n2, na, out, sems):
    flip = place[0]
    copies = []
    for j in range(FACE):
        copies.append((n1.at[j], out.at[j ^ flip, pl.ds(0, ROWS)]))
        copies.append((n2.at[j], out.at[j ^ flip, pl.ds(ROWS, ROWS)]))
        copies.append((na.at[j], out.at[(j + FACE) ^ flip]))
    copies = [
        pltpu.make_async_copy(source, target, sems.at[i])
        for i, (source, target) in enumerate(copies)
    ]
    for copy in copies:
        copy.start()
    for copy in copies:
        copy.wait()


def image_kernel(place, image, received, out):
    for j in range(PLANES):
        at = j ^ place[0]
        total = image[at]
        for step in range(received.shape[1]):
            product = received[0, step, j]
            for group in range(1, GROUPS):
                product = product * received[group, step, j]
            total = total + product
        out[at] = total


def local(pressure_prev, pressure_now, regions, speed_table, image, box):
    prev = pressure_prev[0]
    now = pressure_now[0]
    odd = lax.rem(lax.axis_index("space"), 2)
    place = jnp.stack([7 * odd, 3 * odd]).astype(jnp.int32)
    count = lax.axis_size("space")
    inside = [(i, i ^ 1) for i in range(count)]
    across = [(i, i + 1) for i in range(1, count - 1, 2)]
    across = across + [(j, i) for i, j in across]
    half_shape = (FACE, ROWS, NZ)
    face_shape = (FACE, NY, NZ)
    slab_shape = (PLANES, NY, NZ)
    zone_rows = (ZY // GROUPS, ZZ)
    slab = pltpu.VMEM(slab_shape, F32)
    work = [slab, pltpu.VMEM((NY, 3 * NY), BF16), pltpu.VMEM((3 * NZ, NZ), BF16)]

    def swap_faces(halves):
        return [lax.ppermute(half, "space", across) for half in halves]

    beyond = swap_faces(
        lax.dynamic_slice(now, (4 * odd, half * ROWS, 0), half_shape) for half in range(HALVES)
    )
    halo = lax.ppermute(
        lax.dynamic_slice(now, (4 - 4 * odd, 0, 0), face_shape), "space", inside
    )
    coef, base, rest = call(
        first_kernel,
        [slab_shape] + [face_shape] * 2,
        [SM, SM] + [VM] * 3,
        [VM] * 3,
        (place, speed_table, now, prev, regions),
        scratch=work,
    )
    older = [now]
    zones = ()
    for step in range(STEPS - 1):
        n1 = call(
            functools.partial(face_kernel, 0, step == 0),
            [half_shape],
            [SM] + [VM] * 3,
            [VM],
            (place, base, coef, beyond[0]),
        )[0]
        n2, rest = call(
            functools.partial(face_kernel, 1, step == 0),
            [half_shape, face_shape],
            [SM] + [VM] * 3 + [ANY] * 2,
            [VM, ANY],
            (place, base, coef, beyond[1], rest, n1),
            cost=COST[1],
            aliases={4: 1},
        )
        beyond = swap_faces([n1, n2])
        full, base, rest, zone = call(
            functools.partial(middle_kernel, step == 0),
            [face_shape] * 3 + [(GROUPS, step + 1, PLANES) + zone_rows],
            [SM, SM] + [VM] * (5 + len(older) + len(zones)),
            [VM] * 4,
            (place, box, n1, n2, rest, halo, *older, coef, *zones),
            cost=COST[0] if step < STEPS - 2 else COST[2],
            scratch=work,
        )
        zones = (zone,)
        older = (n1, n2, full)
        halo = lax.ppermute(full, "space", inside)
    n1 = call(
        functools.partial(face_kernel, 0, False),
        [half_shape],
        [SM] + [VM] * 3,
        [VM],
        (place, base, coef, beyond[0]),
        cost=COST[3],
    )[0]
    n2, full, zone = call(
        last_kernel,
        [half_shape, face_shape, (GROUPS, STEPS, PLANES) + zone_rows],
        [SM] + [VM] * 7,
        [VM] * 3,
        (box, base, coef, beyond[1], n1, rest, halo, zone),
    )
    received = lax.all_to_all(zone, "group", split_axis=0, concat_axis=0, tiled=True)

    def gather(three):
        return call(
            gather_kernel,
            [slab_shape],
            [SM] + [ANY] * 3,
            [ANY],
            (place, *three),
            scratch=[pltpu.SemaphoreType.DMA((12,))],
        )[0]

    out_prev = gather(older)
    out_now = gather((n1, n2, full))
    total = call(
        image_kernel, [image.shape], [SM] + [VM] * 2, [VM], (place, image, received)
    )[0]
    return (out_prev[None], out_now[None], total)


def solution(mesh):
    placed = (
        P("group", "space", None, None),
        P("group", "space", None, None),
        P("space", None, None),
        P(),
        P("space", "group", None),
        P(),
    )
    return jax.shard_map(
        local,
        mesh=mesh,
        in_specs=placed,
        out_specs=(
            P("group", "space", None, None),
            P("group", "space", None, None),
            P("space", "group", None),
        ),
        check_vma=False,
    )
```

```python
import functools

import jax
import jax.numpy as jnp
from jax import lax
from jax.experimental import pallas as pl
from jax.experimental.pallas import tpu as pltpu
from jax.sharding import PartitionSpec as P

STEPS = 4
SCALE = 5040.0
CENTRE = -3.0 * 14350.0
TAPS = (8064.0, -1008.0, 128.0, -9.0)
PLANES, NY, NZ = 8, 128, 256
FACE = 4
HALVES = 2
ROWS = NY // HALVES
ZY, ZZ = 64, 128
GROUPS = 8
VMEM_LIMIT = 16 * 1024 * 1024
COST = (1, 10**10, 1, 10**10)
F32 = jnp.float32
BF16 = jnp.bfloat16

VM = pl.BlockSpec(memory_space=pltpu.VMEM)
ANY = pl.BlockSpec(memory_space=pl.ANY)


def band(size):
    apart = jnp.abs(
        lax.broadcasted_iota(jnp.int32, (size, size), 0)
        - lax.broadcasted_iota(jnp.int32, (size, size), 1)
    )
    matrix = jnp.zeros((size, size), F32)
    for k, tap in enumerate(TAPS, 1):
        matrix = jnp.where(apart == k, tap, matrix)
    return matrix.astype(BF16)


def store_bands(across_y, across_z):
    along_y, along_z = band(NY), band(NZ)
    for i in range(3):
        across_y[:, i * NY : (i + 1) * NY] = along_y
        across_z[i * NZ : (i + 1) * NZ, :] = along_z


def call(kernel, outs, in_specs, out_specs, args, cost=1, scratch=(), aliases=None):
    return pl.pallas_call(
        kernel,
        out_shape=[jax.ShapeDtypeStruct(shape, F32) for shape in outs],
        in_specs=in_specs,
        out_specs=out_specs,
        scratch_shapes=list(scratch),
        input_output_aliases=aliases or {},
        compiler_params=pltpu.CompilerParams(vmem_limit_bytes=VMEM_LIMIT),
        cost_estimate=pl.CostEstimate(flops=cost, bytes_accessed=cost, transcendentals=0),
    )(*args)


def flip_of():
    return 7 * lax.rem(lax.axis_index("space"), 2)


def thirds(x):
    high = x.astype(BF16)
    left = x - high.astype(F32)
    middle = left.astype(BF16)
    low = (left - middle.astype(F32)).astype(BF16)
    return high, middle, low


def cross_terms(plane, across_y, across_z):
    pieces = thirds(plane)
    along_z = jnp.dot(
        jnp.concatenate(pieces, axis=1), across_z, preferred_element_type=F32
    )
    along_y = jnp.dot(
        across_y, jnp.concatenate(pieces, axis=0), preferred_element_type=F32
    )
    return along_z + along_y


def advance(now, older, coef_of, cross, store_base, store_next):
    for half in range(HALVES):
        for block in range(ROWS // 8):
            inner = pl.ds(block * 8, 8)
            outer = pl.ds(half * ROWS + block * 8, 8)
            at = (inner, outer, half)
            values = [now(j, at) for j in range(PLANES)]
            for j in range(PLANES):
                total = cross[j, outer, :] + CENTRE * values[j]
                for k, tap in enumerate(TAPS, 1):
                    pair = [values[i] for i in (j + k, j - k) if 0 <= i < len(values)]
                    if pair:
                        total = total + tap * sum(pair[1:], pair[0])
                value = 2.0 * values[j] - older(j, at) + coef_of(j, at) * total
                if j < FACE:
                    store_base(j, at, value)
                else:
                    store_next(j - FACE, at, value)


def from_natural(ref, flip):
    return lambda j, at: ref[j ^ flip, at[1], :]


def from_parts(first, second, rest):
    def rows(j, at):
        if j >= FACE:
            return rest[j - FACE, at[1], :]
        return (first, second)[at[2]][j, at[0], :]

    return rows


def whole_plane(first, second, rest, j):
    if j >= FACE:
        return rest[j - FACE]
    return jnp.concatenate([first[j], second[j]], axis=0)


def first_cell(box_ref):
    return [jnp.max(box_ref[i]).astype(jnp.int32) for i in range(2)]


def cut_zone(plane, box):
    moved = pltpu.roll(plane, (NZ - box[1]) % NZ, 1)[:, :ZZ]
    return pltpu.roll(moved, (NY - box[0]) % NY, 0)[:ZY]


def split_zone(plane, box):
    return cut_zone(plane, box).reshape(GROUPS, ZY // GROUPS, ZZ)


def put_rows(ref):
    def put(j, at, value):
        ref[j, at[1], :] = value

    return put


def first_kernel(
    table_ref, now, prev, regions, coef, base, rest, cross, across_y, across_z, table, sem
):
    load = pltpu.make_async_copy(table_ref, table, sem)
    load.start()
    flip = flip_of()
    store_bands(across_y, across_z)
    for j in range(PLANES):
        cross[j] = cross_terms(now[j ^ flip], across_y[...], across_z[...])
    load.wait()
    scaled = [table[i] * (1.0 / SCALE) for i in range(16)]

    def coef_of(j, at):
        code = regions[j ^ flip, at[1], :]
        level = scaled
        for bit in range(4):
            odd = (code & (1 << bit)) != 0
            level = [
                jnp.where(odd, level[2 * i + 1], level[2 * i]) for i in range(len(level) // 2)
            ]
        coef[j, at[1], :] = level[0]
        return level[0]

    advance(
        from_natural(now, flip),
        from_natural(prev, flip),
        coef_of,
        cross,
        put_rows(base),
        put_rows(rest),
    )


def middle_kernel(first, box_ref, n1, n2, partial, halo, *refs):
    *refs, now, base, nxt, zones, cross, across_y, across_z = refs
    box = first_cell(box_ref)
    if first:
        prev, coef = refs
        older = from_natural(prev, flip_of())
        earlier = ()
    else:
        p1, p2, pa, coef, *earlier = refs
        older = from_parts(p1, p2, pa)
    for zone in earlier:
        zones[:, : zone.shape[1]] = zone[...]
    far_terms(coef, partial, halo, 3 & ~flip_of() if first else 0, now)
    store_bands(across_y, across_z)
    for j in range(PLANES):
        cross[j] = cross_terms(whole_plane(n1, n2, now, j), across_y[...], across_z[...])
    for j in range(PLANES):
        zones[:, zones.shape[1] - 1, j] = split_zone(whole_plane(n1, n2, now, j), box)
    advance(
        from_parts(n1, n2, now),
        older,
        lambda j, at: coef[j, at[1], :],
        cross,
        put_rows(base),
        put_rows(nxt),
    )


def face_terms(base, coef, halo, turn, half, put):
    for block in range(ROWS // 8):
        inner = pl.ds(block * 8, 8)
        outer = pl.ds(half * ROWS + block * 8, 8)
        beyond = [halo[k ^ turn, inner, :] for k in range(FACE)]
        for j in range(FACE):
            total = TAPS[j] * beyond[0]
            for k in range(1, FACE - j):
                total = total + TAPS[j + k] * beyond[k]
            put(j, inner, base[j, outer, :] + coef[j, outer, :] * total)


def face_kernel(half, first, base, coef, halo, *refs):
    out = refs[2 if half else 0]
    turn = 3 & ~flip_of() if first else 0

    def put(j, inner, value):
        out[j, inner, :] = value

    face_terms(base, coef, halo, turn, half, put)


def far_terms(coef, partial, halo, turn, out):
    for block in range(NY // 8):
        rows = pl.ds(block * 8, 8)
        beyond = [halo[(FACE - 1 - k) ^ turn, rows, :] for k in range(FACE)]
        for j in range(FACE):
            total = TAPS[j] * beyond[0]
            for k in range(1, FACE - j):
                total = total + TAPS[j + k] * beyond[k]
            mine = FACE - 1 - j
            out[mine, rows, :] = partial[mine, rows, :] + coef[FACE + mine, rows, :] * total


def last_kernel(
    box_ref, base, coef, halo, n1, partial, far_halo, earlier, n2, now, zones
):
    box = first_cell(box_ref)

    def put(j, inner, value):
        n2[j, inner, :] = value

    face_terms(base, coef, halo, 0, 1, put)
    far_terms(coef, partial, far_halo, 0, now)
    zones[:, : STEPS - 1] = earlier[...]
    for j in range(PLANES):
        zones[:, STEPS - 1, j] = split_zone(whole_plane(n1, n2, now, j), box)


def gather_kernel(n1, n2, na, out, sems):
    flip = flip_of()
    copies = []
    for j in range(FACE):
        copies.append((n1.at[j], out.at[j ^ flip, pl.ds(0, ROWS)]))
        copies.append((n2.at[j], out.at[j ^ flip, pl.ds(ROWS, ROWS)]))
        copies.append((na.at[j], out.at[(j + FACE) ^ flip]))
    copies = [
        pltpu.make_async_copy(source, target, sems.at[i])
        for i, (source, target) in enumerate(copies)
    ]
    for copy in copies:
        copy.start()
    for copy in copies:
        copy.wait()


def image_kernel(image, received, out):
    for j in range(PLANES):
        at = j ^ flip_of()
        total = image[at]
        for step in range(received.shape[1]):
            product = received[0, step, j]
            for group in range(1, GROUPS):
                product = product * received[group, step, j]
            total = total + product
        out[at] = total


def local(pressure_prev, pressure_now, regions, speed_table, image, box):
    prev = pressure_prev[0]
    now = pressure_now[0]
    odd = lax.rem(lax.axis_index("space"), 2)
    count = lax.axis_size("space")
    inside = [(i, i ^ 1) for i in range(count)]
    across = [(i, i + 1) for i in range(1, count - 1, 2)]
    across = across + [(j, i) for i, j in across]
    half_shape = (FACE, ROWS, NZ)
    face_shape = (FACE, NY, NZ)
    slab_shape = (PLANES, NY, NZ)
    zone_rows = (ZY // GROUPS, ZZ)
    slab = pltpu.VMEM(slab_shape, F32)
    box = jnp.broadcast_to(box.astype(F32)[:, None, None], (2, 8, 128))
    work = [slab, pltpu.VMEM((NY, 3 * NY), BF16), pltpu.VMEM((3 * NZ, NZ), BF16)]

    def swap_faces(halves):
        return [lax.ppermute(half, "space", across) for half in halves]

    beyond = swap_faces(
        lax.dynamic_slice(now, (4 * odd, half * ROWS, 0), half_shape) for half in range(HALVES)
    )
    halo = lax.ppermute(
        lax.dynamic_slice(now, (4 - 4 * odd, 0, 0), face_shape), "space", inside
    )
    coef, base, rest = call(
        first_kernel,
        [slab_shape] + [face_shape] * 2,
        [ANY] + [VM] * 3,
        [VM] * 3,
        (speed_table, now, prev, regions),
        scratch=work + [pltpu.SMEM(speed_table.shape, F32), pltpu.SemaphoreType.DMA(())],
    )
    older = [now]
    zones = ()
    for step in range(STEPS - 1):
        n1 = call(
            functools.partial(face_kernel, 0, step == 0),
            [half_shape],
            [VM] * 3,
            [VM],
            (base, coef, beyond[0]),
        )[0]
        n2, rest = call(
            functools.partial(face_kernel, 1, step == 0),
            [half_shape, face_shape],
            [VM] * 3 + [ANY] * 2,
            [VM, ANY],
            (base, coef, beyond[1], rest, n1),
            cost=COST[1],
            aliases={3: 1},
        )
        beyond = swap_faces([n1, n2])
        full, base, rest, zone = call(
            functools.partial(middle_kernel, step == 0),
            [face_shape] * 3 + [(GROUPS, step + 1, PLANES) + zone_rows],
            [VM] * (6 + len(older) + len(zones)),
            [VM] * 4,
            (box, n1, n2, rest, halo, *older, coef, *zones),
            cost=COST[0] if step < STEPS - 2 else COST[2],
            scratch=work,
        )
        zones = (zone,)
        older = (n1, n2, full)
        halo = lax.ppermute(full, "space", inside)
    n1 = call(
        functools.partial(face_kernel, 0, False),
        [half_shape],
        [VM] * 3,
        [VM],
        (base, coef, beyond[0]),
        cost=COST[3],
    )[0]
    n2, full, zone = call(
        last_kernel,
        [half_shape, face_shape, (GROUPS, STEPS, PLANES) + zone_rows],
        [VM] * 8,
        [VM] * 3,
        (box, base, coef, beyond[1], n1, rest, halo, zone),
    )
    received = lax.all_to_all(zone, "group", split_axis=0, concat_axis=0, tiled=True)

    def gather(three):
        return call(
            gather_kernel,
            [slab_shape],
            [ANY] * 3,
            [ANY],
            three,
            scratch=[pltpu.SemaphoreType.DMA((12,))],
        )[0]

    out_prev = gather(older)
    out_now = gather((n1, n2, full))
    total = call(
        image_kernel, [image.shape], [VM] * 2, [VM], (image, received)
    )[0]
    return (out_prev[None], out_now[None], total)


def solution(mesh):
    placed = (
        P("group", "space", None, None),
        P("group", "space", None, None),
        P("space", None, None),
        P(),
        P("space", "group", None),
        P(),
    )
    return jax.shard_map(
        local,
        mesh=mesh,
        in_specs=placed,
        out_specs=(
            P("group", "space", None, None),
            P("group", "space", None, None),
            P("space", "group", None),
        ),
        check_vma=False,
    )
```

```python
import functools

import jax
import jax.numpy as jnp
from jax import lax
from jax.experimental import pallas as pl
from jax.experimental.pallas import tpu as pltpu
from jax.sharding import PartitionSpec as P

STEPS = 4
SCALE = 5040.0
CENTRE = -3.0 * 14350.0
TAPS = (8064.0, -1008.0, 128.0, -9.0)
PLANES, NY, NZ = 8, 128, 256
FACE = 4
FIRST = (0, 64)
ROWS = (64, 64)
ZY, ZZ = 64, 128
GROUPS = 8
VMEM_LIMIT = 16 * 1024 * 1024
COST = (1, 10**10, 1, 10**10)
F32 = jnp.float32
BF16 = jnp.bfloat16

VM = pl.BlockSpec(memory_space=pltpu.VMEM)
ANY = pl.BlockSpec(memory_space=pl.ANY)


def band(size):
    apart = jnp.abs(
        lax.broadcasted_iota(jnp.int32, (size, size), 0)
        - lax.broadcasted_iota(jnp.int32, (size, size), 1)
    )
    matrix = jnp.zeros((size, size), F32)
    for k, tap in enumerate(TAPS, 1):
        matrix = jnp.where(apart == k, tap, matrix)
    return matrix.astype(BF16)


def store_bands(across_y, across_z):
    along_y, along_z = band(NY), band(NZ)
    for i in range(3):
        across_y[:, i * NY : (i + 1) * NY] = along_y
        across_z[i * NZ : (i + 1) * NZ, :] = along_z


def call(kernel, outs, in_specs, out_specs, args, cost=1, scratch=(), aliases=None):
    return pl.pallas_call(
        kernel,
        out_shape=[jax.ShapeDtypeStruct(shape, F32) for shape in outs],
        in_specs=in_specs,
        out_specs=out_specs,
        scratch_shapes=list(scratch),
        input_output_aliases=aliases or {},
        compiler_params=pltpu.CompilerParams(vmem_limit_bytes=VMEM_LIMIT),
        cost_estimate=pl.CostEstimate(flops=cost, bytes_accessed=cost, transcendentals=0),
    )(*args)


def flip_of():
    return 7 * lax.rem(lax.axis_index("space"), 2)


def thirds(x):
    high = x.astype(BF16)
    left = x - high.astype(F32)
    middle = left.astype(BF16)
    low = (left - middle.astype(F32)).astype(BF16)
    return high, middle, low


def cross_terms(plane, across_y, across_z):
    pieces = thirds(plane)
    along_z = jnp.dot(
        jnp.concatenate(pieces, axis=1), across_z, preferred_element_type=F32
    )
    along_y = jnp.dot(
        across_y, jnp.concatenate(pieces, axis=0), preferred_element_type=F32
    )
    return along_z + along_y


def slab_terms(values, j, total):
    total = total + CENTRE * values[j]
    for k, tap in enumerate(TAPS, 1):
        pair = [values[i] for i in (j + k, j - k) if 0 <= i < len(values)]
        if pair:
            total = total + tap * sum(pair[1:], pair[0])
    return total


def advance(now, older, coef_of, cross, store_base, store_next):
    for half in range(len(ROWS)):
        for block in range(ROWS[half] // 8):
            inner = pl.ds(block * 8, 8)
            outer = pl.ds(FIRST[half] + block * 8, 8)
            at = (inner, outer, half)
            values = [now(j, at) for j in range(PLANES)]
            for j in range(PLANES):
                total = slab_terms(values, j, cross[j, outer, :])
                value = 2.0 * values[j] - older(j, at) + coef_of(j, at) * total
                if j < FACE:
                    store_base(j, at, value)
                else:
                    store_next(j - FACE, at, value)


def from_natural(ref, flip):
    return lambda j, at: ref[j ^ flip, at[1], :]


def from_parts(first, second, rest):
    def rows(j, at):
        if j >= FACE:
            return rest[j - FACE, at[1], :]
        return (first, second)[at[2]][j, at[0], :]

    return rows


def whole_plane(first, second, rest, j):
    if j >= FACE:
        return rest[j - FACE]
    return jnp.concatenate([first[j], second[j]], axis=0)


def first_cell(box_ref):
    return [jnp.max(box_ref[i]).astype(jnp.int32) for i in range(2)]


def cut_zone(plane, box):
    moved = pltpu.roll(plane, (NZ - box[1]) % NZ, 1)[:, :ZZ]
    return pltpu.roll(moved, (NY - box[0]) % NY, 0)[:ZY]


def split_zone(plane, box):
    return cut_zone(plane, box).reshape(GROUPS, ZY // GROUPS, ZZ)


def put_rows(ref):
    def put(j, at, value):
        ref[j, at[1], :] = value

    return put


def first_kernel(now, total, across_y, across_z):
    flip = flip_of()
    store_bands(across_y, across_z)
    for j in range(PLANES):
        total[j] = cross_terms(now[j ^ flip], across_y[...], across_z[...])
    for block in range(NY // 8):
        rows = pl.ds(block * 8, 8)
        values = [now[j ^ flip, rows, :] for j in range(PLANES)]
        for j in range(PLANES):
            total[j, rows, :] = slab_terms(values, j, total[j, rows, :])


def second_kernel(table_ref, now, prev, regions, total, coef, base, rest, table, sem):
    load = pltpu.make_async_copy(table_ref, table, sem)
    load.start()
    flip = flip_of()
    load.wait()
    scaled = [table[i] * (1.0 / SCALE) for i in range(16)]
    for j in range(PLANES):
        for block in range(NY // 8):
            rows = pl.ds(block * 8, 8)
            code = regions[j ^ flip, rows, :]
            level = scaled
            for bit in range(4):
                odd = (code & (1 << bit)) != 0
                level = [
                    jnp.where(odd, level[2 * i + 1], level[2 * i]) for i in range(len(level) // 2)
                ]
            coef[j, rows, :] = level[0]
            value = 2.0 * now[j ^ flip, rows, :] - prev[j ^ flip, rows, :] + level[0] * total[j, rows, :]
            if j < FACE:
                base[j, rows, :] = value
            else:
                rest[j - FACE, rows, :] = value


def middle_kernel(first, n1, n2, partial, halo, *refs):
    *refs, now, base, nxt, cross, across_y, across_z = refs
    if first:
        prev, coef = refs
        older = from_natural(prev, flip_of())
    else:
        p1, p2, pa, coef = refs
        older = from_parts(p1, p2, pa)
    far_terms(coef, partial, halo, 3 & ~flip_of() if first else 0, now)
    store_bands(across_y, across_z)
    for j in range(PLANES):
        cross[j] = cross_terms(whole_plane(n1, n2, now, j), across_y[...], across_z[...])
    advance(
        from_parts(n1, n2, now),
        older,
        lambda j, at: coef[j, at[1], :],
        cross,
        put_rows(base),
        put_rows(nxt),
    )


def face_terms(base, coef, halo, turn, half, put):
    for block in range(ROWS[half] // 8):
        inner = pl.ds(block * 8, 8)
        outer = pl.ds(FIRST[half] + block * 8, 8)
        beyond = [halo[k ^ turn, inner, :] for k in range(FACE)]
        for j in range(FACE):
            total = TAPS[j] * beyond[0]
            for k in range(1, FACE - j):
                total = total + TAPS[j + k] * beyond[k]
            put(j, inner, base[j, outer, :] + coef[j, outer, :] * total)


def face_kernel(half, first, base, coef, halo, *refs):
    out = refs[2 if half else 0]
    turn = 3 & ~flip_of() if first else 0

    def put(j, inner, value):
        out[j, inner, :] = value

    face_terms(base, coef, halo, turn, half, put)


def far_terms(coef, partial, halo, turn, out):
    for block in range(NY // 8):
        rows = pl.ds(block * 8, 8)
        beyond = [halo[(FACE - 1 - k) ^ turn, rows, :] for k in range(FACE)]
        for j in range(FACE):
            total = TAPS[j] * beyond[0]
            for k in range(1, FACE - j):
                total = total + TAPS[j + k] * beyond[k]
            mine = FACE - 1 - j
            out[mine, rows, :] = partial[mine, rows, :] + coef[FACE + mine, rows, :] * total


def store_zones(box_ref, pieces, held, sems, zones, step):
    box = first_cell(box_ref)
    for j in range(PLANES):
        held[:, step % held.shape[1], j] = split_zone(whole_plane(*pieces, j), box)
    copy = pltpu.make_async_copy(
        held.at[:, step % held.shape[1]], zones.at[:, step], sems.at[step % held.shape[1]]
    )
    copy.start()
    return copy


def zones_kernel(box_ref, *refs):
    *pieces, zones, held, sems = refs
    copies = [
        store_zones(box_ref, pieces[3 * step : 3 * step + 3], held, sems, zones, step)
        for step in range(STEPS - 1)
    ]
    for copy in copies:
        copy.wait()


def last_kernel(
    box_ref, base, coef, halo, n1, partial, far_halo, earlier, n2, now, zones, held, sems
):
    del earlier

    def put(j, inner, value):
        n2[j, inner, :] = value

    face_terms(base, coef, halo, 0, 1, put)
    far_terms(coef, partial, far_halo, 0, now)
    store_zones(box_ref, (n1, n2, now), held, sems, zones, STEPS - 1).wait()


def gather_kernel(n1, n2, na, out, sems):
    flip = flip_of()
    copies = []
    for j in range(FACE):
        copies.append((n1.at[j], out.at[j ^ flip, pl.ds(FIRST[0], ROWS[0])]))
        copies.append((n2.at[j], out.at[j ^ flip, pl.ds(FIRST[1], ROWS[1])]))
        copies.append((na.at[j], out.at[(j + FACE) ^ flip]))
    copies = [
        pltpu.make_async_copy(source, target, sems.at[i])
        for i, (source, target) in enumerate(copies)
    ]
    for copy in copies:
        copy.start()
    for copy in copies:
        copy.wait()


def image_kernel(image, received, out):
    for j in range(PLANES):
        at = j ^ flip_of()
        total = image[at]
        for step in range(received.shape[1]):
            product = received[0, step, j]
            for group in range(1, GROUPS):
                product = product * received[group, step, j]
            total = total + product
        out[at] = total


def local(pressure_prev, pressure_now, regions, speed_table, image, box):
    prev = pressure_prev[0]
    now = pressure_now[0]
    odd = lax.rem(lax.axis_index("space"), 2)
    count = lax.axis_size("space")
    inside = [(i, i ^ 1) for i in range(count)]
    across = [(i, i + 1) for i in range(1, count - 1, 2)]
    across = across + [(j, i) for i, j in across]
    part_shapes = [(FACE, rows, NZ) for rows in ROWS]
    face_shape = (FACE, NY, NZ)
    slab_shape = (PLANES, NY, NZ)
    zone_rows = (ZY // GROUPS, ZZ)
    slab = pltpu.VMEM(slab_shape, F32)
    box = jnp.broadcast_to(box.astype(F32)[:, None, None], (2, 8, 128))
    work = [slab, pltpu.VMEM((NY, 3 * NY), BF16), pltpu.VMEM((3 * NZ, NZ), BF16)]

    def swap_faces(halves):
        return [lax.ppermute(half, "space", across) for half in halves]

    beyond = swap_faces(
        lax.dynamic_slice(now, (4 * odd, first, 0), shape)
        for first, shape in zip(FIRST, part_shapes)
    )
    halo = lax.ppermute(
        lax.dynamic_slice(now, (4 - 4 * odd, 0, 0), face_shape), "space", inside
    )
    total = call(
        first_kernel,
        [slab_shape],
        [VM],
        [VM],
        (now,),
        scratch=work[1:],
    )[0]
    coef, base, rest = call(
        second_kernel,
        [slab_shape] + [face_shape] * 2,
        [ANY] + [VM] * 4,
        [VM] * 3,
        (speed_table, now, prev, regions, total),
        scratch=[pltpu.SMEM(speed_table.shape, F32), pltpu.SemaphoreType.DMA(())],
    )
    older = [now]
    levels = ()
    for step in range(STEPS - 1):
        n1 = call(
            functools.partial(face_kernel, 0, step == 0),
            part_shapes[:1],
            [VM] * 3,
            [VM],
            (base, coef, beyond[0]),
        )[0]
        n2, rest = call(
            functools.partial(face_kernel, 1, step == 0),
            [part_shapes[1], face_shape],
            [VM] * 3 + [ANY] * 2,
            [VM, ANY],
            (base, coef, beyond[1], rest, n1),
            cost=COST[1],
            aliases={3: 1},
        )
        beyond = swap_faces([n1, n2])
        full, base, rest = call(
            functools.partial(middle_kernel, step == 0),
            [face_shape] * 3,
            [VM] * (5 + len(older)),
            [VM] * 3,
            (n1, n2, rest, halo, *older, coef),
            cost=COST[0] if step < STEPS - 2 else COST[2],
            scratch=work,
        )
        older = (n1, n2, full)
        levels += older
        halo = lax.ppermute(full, "space", inside)
    n1 = call(
        functools.partial(face_kernel, 0, False),
        part_shapes[:1],
        [VM] * 3,
        [VM],
        (base, coef, beyond[0]),
        cost=COST[3],
    )[0]
    zones = call(
        zones_kernel,
        [(GROUPS, STEPS, PLANES) + zone_rows],
        [VM] * (1 + len(levels)),
        [ANY],
        (box, *levels),
        scratch=[
            pltpu.VMEM((GROUPS, STEPS - 1, PLANES) + zone_rows, F32),
            pltpu.SemaphoreType.DMA((STEPS - 1,)),
        ],
    )[0]
    n2, full, zones = call(
        last_kernel,
        [part_shapes[1], face_shape, zones.shape],
        [VM] * 7 + [ANY],
        [VM] * 2 + [ANY],
        (box, base, coef, beyond[1], n1, rest, halo, zones),
        aliases={7: 2},
        scratch=[
            pltpu.VMEM((GROUPS, 1, PLANES) + zone_rows, F32),
            pltpu.SemaphoreType.DMA((1,)),
        ],
    )
    received = lax.all_to_all(zones, "group", split_axis=0, concat_axis=0, tiled=True)

    def gather(three):
        return call(
            gather_kernel,
            [slab_shape],
            [ANY] * 3,
            [ANY],
            three,
            scratch=[pltpu.SemaphoreType.DMA((12,))],
        )[0]

    out_prev = gather(older)
    out_now = gather((n1, n2, full))
    total = call(
        image_kernel, [image.shape], [VM] * 2, [VM], (image, received)
    )[0]
    return (out_prev[None], out_now[None], total)


def solution(mesh):
    placed = (
        P("group", "space", None, None),
        P("group", "space", None, None),
        P("space", None, None),
        P(),
        P("space", "group", None),
        P(),
    )
    return jax.shard_map(
        local,
        mesh=mesh,
        in_specs=placed,
        out_specs=(
            P("group", "space", None, None),
            P("group", "space", None, None),
            P("space", "group", None),
        ),
        check_vma=False,
    )
```

```python
import functools

import jax
import jax.numpy as jnp
from jax import lax
from jax.experimental import pallas as pl
from jax.experimental.pallas import tpu as pltpu
from jax.sharding import PartitionSpec as P

STEPS = 4
SCALE = 5040.0
CENTRE = -3.0 * 14350.0
TAPS = (8064.0, -1008.0, 128.0, -9.0)
PLANES, NY, NZ = 8, 128, 256
FACE = 4
FIRST = (0, 64)
ROWS = (64, 64)
ZY, ZZ = 64, 128
GROUPS = 8
VMEM_LIMIT = 16 * 1024 * 1024
COST = (1, 10**10, 1, 10**10)
F32 = jnp.float32
BF16 = jnp.bfloat16

VM = pl.BlockSpec(memory_space=pltpu.VMEM)
ANY = pl.BlockSpec(memory_space=pl.ANY)


def band(size):
    apart = jnp.abs(
        lax.broadcasted_iota(jnp.int32, (size, size), 0)
        - lax.broadcasted_iota(jnp.int32, (size, size), 1)
    )
    matrix = jnp.zeros((size, size), F32)
    for k, tap in enumerate(TAPS, 1):
        matrix = jnp.where(apart == k, tap, matrix)
    return matrix.astype(BF16)


def store_bands(across_y, across_z):
    along_y, along_z = band(NY), band(NZ)
    for i in range(3):
        across_y[:, i * NY : (i + 1) * NY] = along_y
        across_z[i * NZ : (i + 1) * NZ, :] = along_z


def call(kernel, outs, in_specs, out_specs, args, cost=1, scratch=(), aliases=None):
    return pl.pallas_call(
        kernel,
        out_shape=[jax.ShapeDtypeStruct(shape, F32) for shape in outs],
        in_specs=in_specs,
        out_specs=out_specs,
        scratch_shapes=list(scratch),
        input_output_aliases=aliases or {},
        compiler_params=pltpu.CompilerParams(vmem_limit_bytes=VMEM_LIMIT),
        cost_estimate=pl.CostEstimate(flops=cost, bytes_accessed=cost, transcendentals=0),
    )(*args)


def flip_of():
    return 7 * lax.rem(lax.axis_index("space"), 2)


def thirds(x):
    high = x.astype(BF16)
    left = x - high.astype(F32)
    middle = left.astype(BF16)
    low = (left - middle.astype(F32)).astype(BF16)
    return high, middle, low


def cross_terms(plane, across_y, across_z):
    pieces = thirds(plane)
    along_z = jnp.dot(
        jnp.concatenate(pieces, axis=1), across_z, preferred_element_type=F32
    )
    along_y = jnp.dot(
        across_y, jnp.concatenate(pieces, axis=0), preferred_element_type=F32
    )
    return along_z + along_y


def slab_terms(values, j, total):
    total = total + CENTRE * values[j]
    for k, tap in enumerate(TAPS, 1):
        pair = [values[i] for i in (j + k, j - k) if 0 <= i < len(values)]
        if pair:
            total = total + tap * sum(pair[1:], pair[0])
    return total


def advance(now, older, coef_of, cross, store_base, store_next):
    for half in range(len(ROWS)):
        for block in range(ROWS[half] // 8):
            inner = pl.ds(block * 8, 8)
            outer = pl.ds(FIRST[half] + block * 8, 8)
            at = (inner, outer, half)
            values = [now(j, at) for j in range(PLANES)]
            for j in range(PLANES):
                total = slab_terms(values, j, cross[j, outer, :])
                value = 2.0 * values[j] - older(j, at) + coef_of(j, at) * total
                if j < FACE:
                    store_base(j, at, value)
                else:
                    store_next(j - FACE, at, value)


def from_natural(ref, flip):
    return lambda j, at: ref[j ^ flip, at[1], :]


def from_parts(first, second, rest):
    def rows(j, at):
        if j >= FACE:
            return rest[j - FACE, at[1], :]
        return (first, second)[at[2]][j, at[0], :]

    return rows


def whole_plane(first, second, rest, j):
    if j >= FACE:
        return rest[j - FACE]
    return jnp.concatenate([first[j], second[j]], axis=0)


def first_cell(box_ref):
    return [jnp.max(box_ref[i]).astype(jnp.int32) for i in range(2)]


def cut_zone(plane, box):
    moved = pltpu.roll(plane, (NZ - box[1]) % NZ, 1)[:, :ZZ]
    return pltpu.roll(moved, (NY - box[0]) % NY, 0)[:ZY]


def split_zone(plane, box):
    return cut_zone(plane, box).reshape(GROUPS, ZY // GROUPS, ZZ)


def put_rows(ref):
    def put(j, at, value):
        ref[j, at[1], :] = value

    return put


def first_kernel(now, total, across_y, across_z):
    flip = flip_of()
    store_bands(across_y, across_z)
    for j in range(PLANES):
        total[j] = cross_terms(now[j ^ flip], across_y[...], across_z[...])
    for block in range(NY // 8):
        rows = pl.ds(block * 8, 8)
        values = [now[j ^ flip, rows, :] for j in range(PLANES)]
        for j in range(PLANES):
            total[j, rows, :] = slab_terms(values, j, total[j, rows, :])


def second_kernel(table_ref, now, prev, regions, total, coef, base, rest, table, sem):
    load = pltpu.make_async_copy(table_ref, table, sem)
    load.start()
    flip = flip_of()
    load.wait()
    scaled = [table[i] * (1.0 / SCALE) for i in range(16)]
    for j in range(PLANES):
        for block in range(NY // 8):
            rows = pl.ds(block * 8, 8)
            code = regions[j ^ flip, rows, :]
            level = scaled
            for bit in range(4):
                odd = (code & (1 << bit)) != 0
                level = [
                    jnp.where(odd, level[2 * i + 1], level[2 * i]) for i in range(len(level) // 2)
                ]
            coef[j, rows, :] = level[0]
            value = 2.0 * now[j ^ flip, rows, :] - prev[j ^ flip, rows, :] + level[0] * total[j, rows, :]
            if j < FACE:
                base[j, rows, :] = value
            else:
                rest[j - FACE, rows, :] = value


def middle_kernel(first, n1, n2, partial, halo, *refs):
    *refs, now, base, nxt, cross, across_y, across_z = refs
    if first:
        prev, coef = refs
        older = from_natural(prev, flip_of())
    else:
        p1, p2, pa, coef = refs
        older = from_parts(p1, p2, pa)
    far_terms(coef, partial, halo, 3 & ~flip_of() if first else 0, now)
    store_bands(across_y, across_z)
    for j in range(PLANES):
        cross[j] = cross_terms(whole_plane(n1, n2, now, j), across_y[...], across_z[...])
    advance(
        from_parts(n1, n2, now),
        older,
        lambda j, at: coef[j, at[1], :],
        cross,
        put_rows(base),
        put_rows(nxt),
    )


def face_terms(base, coef, halo, turn, half, put):
    for block in range(ROWS[half] // 8):
        inner = pl.ds(block * 8, 8)
        outer = pl.ds(FIRST[half] + block * 8, 8)
        beyond = [halo[k ^ turn, inner, :] for k in range(FACE)]
        for j in range(FACE):
            total = TAPS[j] * beyond[0]
            for k in range(1, FACE - j):
                total = total + TAPS[j + k] * beyond[k]
            put(j, inner, base[j, outer, :] + coef[j, outer, :] * total)


def face_kernel(half, first, base, coef, halo, *refs):
    out = refs[2 if half else 0]
    turn = 3 & ~flip_of() if first else 0

    def put(j, inner, value):
        out[j, inner, :] = value

    face_terms(base, coef, halo, turn, half, put)


def far_terms(coef, partial, halo, turn, out):
    for block in range(NY // 8):
        rows = pl.ds(block * 8, 8)
        beyond = [halo[(FACE - 1 - k) ^ turn, rows, :] for k in range(FACE)]
        for j in range(FACE):
            total = TAPS[j] * beyond[0]
            for k in range(1, FACE - j):
                total = total + TAPS[j + k] * beyond[k]
            mine = FACE - 1 - j
            out[mine, rows, :] = partial[mine, rows, :] + coef[FACE + mine, rows, :] * total


def zones_kernel(box_ref, coef, partial, far_halo, *refs):
    *pieces, now, zones, held, sems = refs
    box = first_cell(box_ref)
    copies = []
    for step in range(STEPS):
        if step < STEPS - 1:
            planes = [whole_plane(*pieces[3 * step : 3 * step + 3], j) for j in range(PLANES)]
        else:
            far_terms(coef, partial, far_halo, 0, now)
            planes = [now[j] for j in range(FACE)]
        cut = pl.ds(PLANES - len(planes), len(planes))
        for j, plane in enumerate(planes, PLANES - len(planes)):
            held[:, step, j] = split_zone(plane, box)
        copies.append(
            pltpu.make_async_copy(held.at[:, step, cut], zones.at[:, step, cut], sems.at[step])
        )
        copies[-1].start()
    for copy in copies:
        copy.wait()


def last_kernel(box_ref, base, coef, halo, n1, earlier, n2, zones, held, sem):
    del earlier
    box = first_cell(box_ref)

    def put(j, inner, value):
        n2[j, inner, :] = value

    face_terms(base, coef, halo, 0, 1, put)
    for j in range(FACE):
        held[:, j] = split_zone(jnp.concatenate([n1[j], n2[j]], axis=0), box)
    copy = pltpu.make_async_copy(held, zones.at[:, STEPS - 1, pl.ds(0, FACE)], sem)
    copy.start()
    copy.wait()


def gather_kernel(n1, n2, na, out, sems):
    flip = flip_of()
    copies = []
    for j in range(FACE):
        copies.append((n1.at[j], out.at[j ^ flip, pl.ds(FIRST[0], ROWS[0])]))
        copies.append((n2.at[j], out.at[j ^ flip, pl.ds(FIRST[1], ROWS[1])]))
        copies.append((na.at[j], out.at[(j + FACE) ^ flip]))
    copies = [
        pltpu.make_async_copy(source, target, sems.at[i])
        for i, (source, target) in enumerate(copies)
    ]
    for copy in copies:
        copy.start()
    for copy in copies:
        copy.wait()


def image_kernel(image, received, out):
    for j in range(PLANES):
        at = j ^ flip_of()
        total = image[at]
        for step in range(received.shape[1]):
            product = received[0, step, j]
            for group in range(1, GROUPS):
                product = product * received[group, step, j]
            total = total + product
        out[at] = total


def local(pressure_prev, pressure_now, regions, speed_table, image, box):
    prev = pressure_prev[0]
    now = pressure_now[0]
    odd = lax.rem(lax.axis_index("space"), 2)
    count = lax.axis_size("space")
    inside = [(i, i ^ 1) for i in range(count)]
    across = [(i, i + 1) for i in range(1, count - 1, 2)]
    across = across + [(j, i) for i, j in across]
    part_shapes = [(FACE, rows, NZ) for rows in ROWS]
    face_shape = (FACE, NY, NZ)
    slab_shape = (PLANES, NY, NZ)
    zone_rows = (ZY // GROUPS, ZZ)
    slab = pltpu.VMEM(slab_shape, F32)
    box = jnp.broadcast_to(box.astype(F32)[:, None, None], (2, 8, 128))
    work = [slab, pltpu.VMEM((NY, 3 * NY), BF16), pltpu.VMEM((3 * NZ, NZ), BF16)]

    def swap_faces(halves):
        return [lax.ppermute(half, "space", across) for half in halves]

    beyond = swap_faces(
        lax.dynamic_slice(now, (4 * odd, first, 0), shape)
        for first, shape in zip(FIRST, part_shapes)
    )
    halo = lax.ppermute(
        lax.dynamic_slice(now, (4 - 4 * odd, 0, 0), face_shape), "space", inside
    )
    total = call(
        first_kernel,
        [slab_shape],
        [VM],
        [VM],
        (now,),
        scratch=work[1:],
    )[0]
    coef, base, rest = call(
        second_kernel,
        [slab_shape] + [face_shape] * 2,
        [ANY] + [VM] * 4,
        [VM] * 3,
        (speed_table, now, prev, regions, total),
        scratch=[pltpu.SMEM(speed_table.shape, F32), pltpu.SemaphoreType.DMA(())],
    )
    older = [now]
    levels = ()
    for step in range(STEPS - 1):
        n1 = call(
            functools.partial(face_kernel, 0, step == 0),
            part_shapes[:1],
            [VM] * 3,
            [VM],
            (base, coef, beyond[0]),
        )[0]
        n2, rest = call(
            functools.partial(face_kernel, 1, step == 0),
            [part_shapes[1], face_shape],
            [VM] * 3 + [ANY] * 2,
            [VM, ANY],
            (base, coef, beyond[1], rest, n1),
            cost=COST[1],
            aliases={3: 1},
        )
        beyond = swap_faces([n1, n2])
        full, base, rest = call(
            functools.partial(middle_kernel, step == 0),
            [face_shape] * 3,
            [VM] * (5 + len(older)),
            [VM] * 3,
            (n1, n2, rest, halo, *older, coef),
            cost=COST[0] if step < STEPS - 2 else COST[2],
            scratch=work,
        )
        older = (n1, n2, full)
        levels += older
        halo = lax.ppermute(full, "space", inside)
    n1 = call(
        functools.partial(face_kernel, 0, False),
        part_shapes[:1],
        [VM] * 3,
        [VM],
        (base, coef, beyond[0]),
        cost=COST[3],
    )[0]
    zone_shape = (GROUPS, STEPS, PLANES) + zone_rows
    full, zones = call(
        zones_kernel,
        [face_shape, zone_shape],
        [VM] * (4 + len(levels)),
        [VM, ANY],
        (box, coef, rest, halo, *levels),
        scratch=[pltpu.VMEM(zone_shape, F32), pltpu.SemaphoreType.DMA((STEPS,))],
    )
    n2, zones = call(
        last_kernel,
        [part_shapes[1], zone_shape],
        [VM] * 5 + [ANY],
        [VM, ANY],
        (box, base, coef, beyond[1], n1, zones),
        aliases={5: 1},
        scratch=[
            pltpu.VMEM((GROUPS, FACE) + zone_rows, F32),
            pltpu.SemaphoreType.DMA(()),
        ],
    )
    received = lax.all_to_all(zones, "group", split_axis=0, concat_axis=0, tiled=True)

    def gather(three):
        return call(
            gather_kernel,
            [slab_shape],
            [ANY] * 3,
            [ANY],
            three,
            scratch=[pltpu.SemaphoreType.DMA((12,))],
        )[0]

    out_prev = gather(older)
    out_now = gather((n1, n2, full))
    total = call(
        image_kernel, [image.shape], [VM] * 2, [VM], (image, received)
    )[0]
    return (out_prev[None], out_now[None], total)


def solution(mesh):
    placed = (
        P("group", "space", None, None),
        P("group", "space", None, None),
        P("space", None, None),
        P(),
        P("space", "group", None),
        P(),
    )
    return jax.shard_map(
        local,
        mesh=mesh,
        in_specs=placed,
        out_specs=(
            P("group", "space", None, None),
            P("group", "space", None, None),
            P("space", "group", None),
        ),
        check_vma=False,
    )
```
